32 devices in a mesh: blk: 16 (over z, y, core), grp: 2 (over x).
Axes of the slice: x: 2, y: 2, z: 4, core: 2. Of those that a mesh axis runs over, the one named last changes fastest.
Arguments:
- orbitals: float32 [8192, 512], P('blk'), may hold values from -6 to 6
- points: float32 [3, 8192], P(None, 'blk'), may hold values from 0 to 1
Outputs:
- exchange_vectors: float32 [8192, 512], P('blk')
The draws below stay inside these ranges and needn't reach their ends.
All inputs are finite; a program needn't handle non-finite values.
Results may differ from the reference program's by a relative error of at most 0.0003.
Values sent between devices are 32-bit elements; how exact they have to be, the bound alone decides.
A program may use at most 64 MiB of HBM per device.

```python
import jax
import jax.numpy as jnp
from jax import lax

PTS_DEV = 512
NORB = 512
POINTS = 8192
N_BLK = 16


def shard_levels(key, shape, shards, least, largest):
    level, own = 1.0, jax.random.fold_in(key, 6)
    for dim, parts in shards:
        steps = jnp.exp(jax.random.uniform(jax.random.fold_in(own, dim), (parts,), jnp.float32, least / len(shards), largest / len(shards)))
        level = level * jnp.repeat(steps, shape[dim] // parts).reshape([-1 if axis == dim else 1 for axis in range(len(shape))])
    return level


def normal_values(key, extent, deviation, reach, shards=(), kind=jnp.bfloat16):
    gain = shard_levels(key, extent, shards, -0.22, 0.18) if shards else 1.0
    result = jax.random.normal(key, extent, jnp.float32) * deviation * gain
    return jnp.minimum(jnp.maximum(result, -reach), reach).astype(kind)


def setup_inputs(seed: int = 0) -> dict:
    streams_of = jax.random.split(jax.random.key(seed), 3)
    return {
        "orbitals": normal_values(streams_of[0], (POINTS, NORB), 1.0, 6.0, ((0, 16),), jnp.float32),
        "points": jnp.clip(1.0 * jax.random.uniform(streams_of[1], (3, POINTS), jnp.float32) ** shard_levels(streams_of[1], (3, POINTS), ((1, 16),), -0.2, 0.2), 0.0, 1.0),
    }


def kernel(near_coords, far_coords):
    squared = jnp.zeros((near_coords.shape[1], far_coords.shape[1]), near_coords.dtype)
    for axis_index in range(3):
        spacing = near_coords[axis_index][:, None] - far_coords[axis_index][None, :]
        squared = squared + spacing * spacing
    return lax.rsqrt(squared + 0.0025)

def reference(orbitals, points):
    point_count = orbitals.shape[0]
    weight = 1.0 / point_count
    highest = lax.Precision.HIGHEST

    def row_block(start_row):
        near_rows = lax.dynamic_slice_in_dim(orbitals, start_row, PTS_DEV, 0)
        near_coords = lax.dynamic_slice_in_dim(points, start_row, PTS_DEV, 1)
        gram_tile = lax.dot_general(near_rows, orbitals, (((1,), (1,)), ((), ())), precision=highest)
        screened = gram_tile * kernel(near_coords, points)
        return -weight * jnp.dot(screened, orbitals, precision=highest)
    starts = (jnp.arange(N_BLK) * PTS_DEV).astype(jnp.int32)
    applied = lax.map(row_block, starts).reshape(point_count, orbitals.shape[1])
    correlation = weight * jnp.dot(orbitals.T, applied, precision=highest)
    factor = jnp.linalg.cholesky(-correlation)
    return lax.linalg.triangular_solve(factor, applied, left_side=False, lower=True, transpose_a=True)
```

```python
import functools

import jax
import jax.numpy as jnp
from jax import lax
from jax.experimental import pallas as pl
from jax.experimental.pallas import tpu as pltpu
from jax.sharding import PartitionSpec as P

MESH = pl.DeviceIdType.MESH
F32 = jnp.float32
BF16 = jnp.bfloat16
HIGHEST = lax.Precision.HIGHEST
PAD = 8


def two_wide(mesh):
    devices = mesh.devices.reshape(mesh.shape["blk"], mesh.shape["grp"])
    if devices.shape[0] < 6:
        return True
    near = getattr(devices[0, 0], "coords", None)
    far = getattr(devices[4, 0], "coords", None)
    if near is None or far is None:
        return True
    return sum(abs(a - b) for a, b in zip(near, far)) == 1


def split(value):
    high = value.astype(BF16)
    return high, (value - high.astype(F32)).astype(BF16)


def dot(a, b, dims):
    return lax.dot_general(a, b, (dims, ((), ())), preferred_element_type=F32)


def dot3(a, b, dims):
    return dot(a[0], b[0], dims) + (dot(a[1], b[0], dims) + dot(a[0], b[1], dims))


def apply_kernel(
    sizes, orb_ref, own_ref, near_ref, applied_ref, corr_ref,
    buf, nh, nl, th, tl, fh, fl, acc, part, half_buf, red, rs_buf, grp_buf, corr_buf, app_buf,
    gather_recv, gather_send, half_sem, rs_send, rs_recv, grp_send, grp_recv,
    ag_recv, ag_send, ag_sib, app_send, app_recv,
):
    n_blk, n_grp, inner_two, weight, tile = sizes
    chips = n_blk // 2
    length = chips // 2
    rows, norb = orb_ref.shape
    piece = own_ref.shape[1] - PAD
    width = 2 * piece
    me = lax.axis_index("blk")
    grp = lax.axis_index("grp")
    core = me % 2
    chip = me // 2

    def chip_at(position):
        side = position // length
        along = side * (2 * length - 1 - 2 * position) + position
        return along * 2 + side if inner_two else side * length + along

    if inner_two:
        side, along = chip % 2, chip // 2
    else:
        side, along = chip // length, chip % length
    place = along + side * (2 * length - 1 - 2 * along)

    def device_at(position, which):
        return chip_at((position + 2 * chips) % chips) * 2 + which

    sibling = me + 1 - 2 * core
    right = device_at(place + 1, core)
    left = device_at(place - 1, core)

    def send(origin, h, kind, target):
        return pltpu.make_async_remote_copy(
            src_ref=buf.at[origin, h], dst_ref=buf.at[origin, h],
            send_sem=gather_send.at[kind, origin, h], recv_sem=gather_recv.at[origin, h],
            device_id={"blk": target}, device_id_type=MESH)

    def arrived(origin, h):
        send(origin, h, 0, right).wait_recv()

    barrier = pltpu.get_barrier_semaphore()
    pl.semaphore_signal(barrier, inc=1, device_id={"blk": sibling}, device_id_type=MESH)
    for j in range(1, chips):
        pl.semaphore_signal(barrier, inc=1, device_id={"blk": device_at(place + j, core)}, device_id_type=MESH)
    for j in range(1, n_grp):
        pl.semaphore_signal(barrier, inc=1, device_id={"grp": (grp + j) % n_grp}, device_id_type=MESH)
    buf[me] = own_ref[...]
    pl.semaphore_wait(barrier, 1 + (chips - 1) + (n_grp - 1))

    for h in range(2):
        send(me, h, 0, right).start()
        send(me, h, 1, left).start()
        send(me, h, 2, sibling).start()

    near_high, near_low = split(orb_ref[...])
    nh[...] = near_high
    nl[...] = near_low
    turned_high, turned_low = split(orb_ref[...].T)
    th[...] = turned_high
    tl[...] = turned_low
    acc[...] = jnp.zeros_like(acc)

    def compute(origin):
        for h in range(2):
            high, low = split(buf[origin, h, :piece, :])
            fh[h * piece:(h + 1) * piece, :] = high
            fl[h * piece:(h + 1) * piece, :] = low
        coords = buf[origin, 0, piece:, :width]
        far = (fh[...], fl[...])

        def rows_of(t, carry):
            here = pl.ds(pl.multiple_of(t * tile, tile), tile)
            gram = dot3((nh[here, :], nl[here, :]), far, ((1,), (1,)))
            squared = jnp.zeros((tile, width), F32)
            for k in range(3):
                spacing = near_ref[here, k:k + 1] - coords[k:k + 1, :]
                squared = squared + spacing * spacing
            screened = split(gram * lax.rsqrt(squared + 0.0025))
            acc[here, :] += dot3(screened, far, ((1,), (0,)))
            return carry

        lax.fori_loop(0, rows // tile, rows_of, 0)

    def first(i, carry):
        origin = jnp.where(i == 0, me, sibling)

        @pl.when(i == 1)
        def _():
            arrived(sibling, 0)
            arrived(sibling, 1)

        compute(origin)
        return carry

    lax.fori_loop(0, 2, first, 0)

    full = (chips - 1) // 2

    def service(d, h):
        for kind, sign, target in ((0, -1, right), (1, 1, left)):
            origin = device_at(place + sign * d, core)
            arrived(origin, h)
            if h == kind:
                send(origin, h, kind, target).start()
            else:
                @pl.when(d < full)
                def _():
                    send(origin, h, kind, target).start()
            send(origin, h, 2, sibling).start()

    def pair(d, which, wait):
        def one(i, carry):
            origin = device_at(place + (2 * i - 1) * d, which)
            if wait:
                arrived(origin, 0)
                arrived(origin, 1)
            compute(origin)
            return carry
        lax.fori_loop(0, 2, one, 0)

    def round_of(d, carry):
        service(d, 0)

        @pl.when(d > 1)
        def _():
            pair(d - 1, 1 - core, True)

        service(d, 1)
        pair(d, core, False)
        return carry

    lax.fori_loop(1, full + 1, round_of, 0)
    pair(full, 1 - core, True)
    across = device_at(place + length, core)
    for h in range(2):
        arrived(across, h)
        send(across, h, 2, sibling).start()

    def last(i, carry):
        origin = device_at(place + length, jnp.where(i == 0, core, 1 - core))

        @pl.when(i == 1)
        def _():
            arrived(origin, 0)
            arrived(origin, 1)

        compute(origin)
        return carry

    lax.fori_loop(0, 2, last, 0)

    app_buf[grp] = -weight * acc[...]

    def app_copy(j):
        return pltpu.make_async_remote_copy(
            src_ref=app_buf.at[grp], dst_ref=app_buf.at[grp],
            send_sem=app_send.at[j], recv_sem=app_recv.at[grp],
            device_id={"grp": (grp + j) % n_grp}, device_id_type=MESH)

    def app_in(j):
        other = (grp + j) % n_grp
        return pltpu.make_async_remote_copy(
            src_ref=app_buf.at[other], dst_ref=app_buf.at[other],
            send_sem=app_send.at[j], recv_sem=app_recv.at[other],
            device_id={"grp": other}, device_id_type=MESH)

    half = norb // 2
    share = half // chips
    scaled = split(acc[...])
    part[...] = (dot3((th[...], tl[...]), scaled, ((1,), (0,))) * (weight * weight)).reshape(part.shape)
    to_sibling = pltpu.make_async_remote_copy(
        src_ref=part.at[1 - core], dst_ref=half_buf, send_sem=half_sem.at[0], recv_sem=half_sem.at[1],
        device_id={"blk": sibling}, device_id_type=MESH)
    to_sibling.start()
    for j in range(1, n_grp):
        app_copy(j).start()
    to_sibling.wait_recv()
    red[...] = (part[core] + half_buf[...]).reshape(red.shape)

    def rs_copy(j):
        to = (place + j) % chips
        return pltpu.make_async_remote_copy(
            src_ref=red.at[to], dst_ref=rs_buf.at[j], send_sem=rs_send.at[j], recv_sem=rs_recv.at[j],
            device_id={"blk": device_at(to, core)}, device_id_type=MESH)

    for j in range(1, chips):
        rs_copy(j).start()
    total = red[place]
    for j in range(1, chips):
        rs_copy(j).wait_recv()
        total = total + rs_buf[j]
    grp_buf[grp] = total

    def grp_copy(j):
        return pltpu.make_async_remote_copy(
            src_ref=grp_buf.at[grp], dst_ref=grp_buf.at[grp],
            send_sem=grp_send.at[j], recv_sem=grp_recv.at[grp],
            device_id={"grp": (grp + j) % n_grp}, device_id_type=MESH)

    def grp_in(j):
        other = (grp + j) % n_grp
        return pltpu.make_async_remote_copy(
            src_ref=grp_buf.at[other], dst_ref=grp_buf.at[other],
            send_sem=grp_send.at[j], recv_sem=grp_recv.at[other],
            device_id={"grp": other}, device_id_type=MESH)

    for j in range(1, n_grp):
        grp_copy(j).start()
    for j in range(1, n_grp):
        grp_in(j).wait_recv()
    total = grp_buf[0]
    for j in range(1, n_grp):
        total = total + grp_buf[j]
    mine = core * chips + place
    corr_buf[mine] = total

    def ag_copy(block, sem, target):
        return pltpu.make_async_remote_copy(
            src_ref=corr_buf.at[block], dst_ref=corr_buf.at[block],
            send_sem=sem, recv_sem=ag_recv.at[block],
            device_id={"blk": target}, device_id_type=MESH)

    for j in range(1, chips):
        ag_copy(mine, ag_send.at[j], device_at(place + j, core)).start()
    ag_copy(mine, ag_sib.at[0], sibling).start()
    for j in range(1, chips):
        block = core * chips + (place + chips - j) % chips
        ag_copy(block, ag_sib.at[j], sibling).wait_recv()
        ag_copy(block, ag_sib.at[j], sibling).start()
    for j in range(chips):
        block = (1 - core) * chips + (place + chips - j) % chips
        ag_copy(block, ag_sib.at[j], sibling).wait_recv()
    corr_ref[...] = corr_buf[...]

    for j in range(1, n_grp):
        app_in(j).wait_recv()
    whole = app_buf[0]
    for j in range(1, n_grp):
        whole = whole + app_buf[j]
    applied_ref[...] = whole

    def sent(d, carry):
        for kind, sign, target in ((0, -1, right), (1, 1, left)):
            origin = device_at(place + sign * d, core)
            for h in range(2):
                if h == kind:
                    send(origin, h, kind, target).wait_send()
                else:
                    @pl.when(d < full)
                    def _():
                        send(origin, h, kind, target).wait_send()
                send(origin, h, 2, sibling).wait_send()
        return carry

    lax.fori_loop(1, full + 1, sent, 0)
    for h in range(2):
        send(me, h, 0, right).wait_send()
        send(me, h, 1, left).wait_send()
        send(me, h, 2, sibling).wait_send()
        send(across, h, 2, sibling).wait_send()
    to_sibling.wait_send()
    for j in range(1, chips):
        rs_copy(j).wait_send()
        ag_copy(mine, ag_send.at[j], device_at(place + j, core)).wait_send()
    for j in range(chips):
        block = core * chips + (place + chips - j) % chips
        ag_copy(block, ag_sib.at[j], sibling).wait_send()
    for j in range(1, n_grp):
        app_copy(j).wait_send()
        grp_copy(j).wait_send()


def solve_kernel(corr_ref, applied_ref, out_ref, a, work):
    norb = corr_ref.shape[0]
    rows = applied_ref.shape[0]
    base = 128
    a[:norb, :] = corr_ref[...]
    a[norb:, :] = applied_ref[...]
    lane = lax.broadcasted_iota(jnp.int32, (8, base), 1)
    sub = lax.broadcasted_iota(jnp.int32, (8, base), 0)
    eye = (lax.broadcasted_iota(jnp.int32, (base, base), 0)
           == lax.broadcasted_iota(jnp.int32, (base, base), 1)).astype(F32)
    for b in range(norb // base):
        here = slice(b * base, (b + 1) * base)
        work[:, :base] = a[here, here]
        work[:, base:] = eye

        def slab(s, carry):
            top = pl.multiple_of(s * 8, 8)
            left = work[pl.ds(top, 8), :base]
            right = work[pl.ds(top, 8), base:]
            rolled = pltpu.roll(left, base - s * 8, axis=1)
            cols = [jnp.broadcast_to(rolled[:, j:j + 1], (8, base)) for j in range(8)]
            scale = jnp.zeros((8, base), F32)
            for j in range(8):
                pivot = jnp.broadcast_to(cols[j][j:j + 1, :], (8, base))
                root = lax.rsqrt(pivot)
                scale = jnp.where(sub == j, root, scale)
                factor = jnp.where(sub > j, cols[j] / pivot, 0.0)
                left = left - factor * left[j:j + 1, :]
                right = right - factor * right[j:j + 1, :]
                for m in range(j + 1, 8):
                    cols[m] = cols[m] - factor * cols[m][j:j + 1, :]
            left = left * scale
            right = right * scale
            work[pl.ds(top, 8), base:] = right
            below = jnp.where(lane >= s * 8 + 8, left, 0.0)
            both = jnp.concatenate([left, right], axis=1)
            work[...] -= lax.dot_general(
                below, both, (((0,), (0,)), ((), ())), precision=HIGHEST, preferred_element_type=F32)
            return carry

        lax.fori_loop(0, base // 8, slab, 0)
        inverse = work[:, base:]
        below = slice((b + 1) * base, norb + rows)
        panel = lax.dot_general(
            a[below, here], inverse, (((1,), (1,)), ((), ())), precision=HIGHEST, preferred_element_type=F32)
        a[below, here] = panel
        for j in range(b + 1, norb // base):
            there = slice(j * base, (j + 1) * base)
            low = slice(j * base, norb + rows)
            a[low, there] -= lax.dot_general(
                a[low, here], a[there, here], (((1,), (1,)), ((), ())),
                precision=HIGHEST, preferred_element_type=F32)
    out_ref[...] = a[norb:, :]


def solution(mesh):
    n_blk, n_grp = mesh.shape["blk"], mesh.shape["grp"]
    inner_two = two_wide(mesh)
    chips = n_blk // 2

    def shards(orbitals, points):
        rows, norb = orbitals.shape
        weight = 1.0 / (rows * n_blk)
        width = rows // n_grp
        piece = width // 2
        start = lax.axis_index("grp") * width
        far_rows = lax.dynamic_slice_in_dim(orbitals, start, width, 0).reshape(2, piece, norb)
        far_coords = lax.dynamic_slice_in_dim(points, start, width, 1)
        far_coords = jnp.pad(far_coords, ((0, PAD - 3), (0, norb - width)))
        own = jnp.concatenate([far_rows, jnp.broadcast_to(far_coords, (2, PAD, norb))], axis=1)
        share = norb // 2 // chips
        vmem = pl.BlockSpec(memory_space=pltpu.VMEM)
        dma = pltpu.SemaphoreType.DMA
        applied, corr = pl.pallas_call(
            functools.partial(apply_kernel, (n_blk, n_grp, inner_two, weight, min(256, rows))),
            out_shape=[jax.ShapeDtypeStruct((rows, norb), F32), jax.ShapeDtypeStruct((n_blk, share, norb), F32)],
            in_specs=[vmem] * 3,
            out_specs=[vmem] * 2,
            scratch_shapes=[
                pltpu.VMEM((n_blk, 2, piece + PAD, norb), F32),
                pltpu.VMEM((rows, norb), BF16), pltpu.VMEM((rows, norb), BF16),
                pltpu.VMEM((norb, rows), BF16), pltpu.VMEM((norb, rows), BF16),
                pltpu.VMEM((width, norb), BF16), pltpu.VMEM((width, norb), BF16),
                pltpu.VMEM((rows, norb), F32),
                pltpu.VMEM((2, norb // 2, norb), F32),
                pltpu.VMEM((norb // 2, norb), F32),
                pltpu.VMEM((chips, share, norb), F32),
                pltpu.VMEM((chips, share, norb), F32),
                pltpu.VMEM((n_grp, share, norb), F32),
                pltpu.VMEM((n_blk, share, norb), F32),
                pltpu.VMEM((n_grp, rows, norb), F32),
                dma((n_blk, 2)), dma((3, n_blk, 2)), dma((2,)), dma((chips,)), dma((chips,)),
                dma((n_grp,)), dma((n_grp,)), dma((n_blk,)), dma((chips,)), dma((chips,)),
                dma((n_grp,)), dma((n_grp,)),
            ],
            compiler_params=pltpu.CompilerParams(
                collective_id=0, has_side_effects=True, vmem_limit_bytes=48 << 20),
            name="apply_and_correlate",
        )(orbitals, own, points.T)
        return pl.pallas_call(
            solve_kernel,
            out_shape=jax.ShapeDtypeStruct((rows, norb), F32),
            in_specs=[vmem] * 2,
            out_specs=vmem,
            scratch_shapes=[pltpu.VMEM((norb + rows, norb), F32), pltpu.VMEM((128, 256), F32)],
            compiler_params=pltpu.CompilerParams(vmem_limit_bytes=32 << 20),
            name="factor_and_solve",
        )(corr.reshape(norb, norb), applied)

    return jax.shard_map(
        shards,
        mesh=mesh,
        in_specs=(P("blk", None), P(None, "blk")),
        out_specs=P("blk", None),
        check_vma=False,
    )
```

```python
import functools

import jax
import jax.numpy as jnp
from jax import lax
from jax.experimental import pallas as pl
from jax.experimental.pallas import tpu as pltpu
from jax.sharding import PartitionSpec as P

MESH = pl.DeviceIdType.MESH
F32 = jnp.float32
BF16 = jnp.bfloat16
HIGHEST = lax.Precision.HIGHEST
PAD = 8
BASE = 128


def two_wide(mesh):
    devices = mesh.devices.reshape(mesh.shape["blk"], mesh.shape["grp"])
    if devices.shape[0] < 6:
        return True
    near = getattr(devices[0, 0], "coords", None)
    far = getattr(devices[4, 0], "coords", None)
    if near is None or far is None:
        return True
    return sum(abs(a - b) for a, b in zip(near, far)) == 1


def split(value):
    high = value.astype(BF16)
    return high, (value - high.astype(F32)).astype(BF16)


def dot(a, b, dims):
    return lax.dot_general(a, b, (dims, ((), ())), preferred_element_type=F32)


def dot3(a, b, dims):
    return dot(a[0], b[0], dims) + (dot(a[1], b[0], dims) + dot(a[0], b[1], dims))


def apply_kernel(
    sizes, orb_ref, own_ref, near_ref, applied_ref, corr_ref,
    buf, near3, turned3, far3, low3, acc, part, half_buf, red, rs_buf, grp_buf, corr_buf, app_buf,
    gather_recv, gather_send, half_sem, rs_send, rs_recv, grp_send, grp_recv,
    ag_recv, ag_send, ag_sib, app_send, app_recv,
):
    n_blk, n_grp, inner_two, weight, tile = sizes
    chips = n_blk // 2
    length = chips // 2
    rows, norb = orb_ref.shape
    piece = own_ref.shape[1] - PAD
    width = 2 * piece
    me = lax.axis_index("blk")
    grp = lax.axis_index("grp")
    core = me % 2
    chip = me // 2

    def chip_at(position):
        side = position // length
        along = side * (2 * length - 1 - 2 * position) + position
        return along * 2 + side if inner_two else side * length + along

    if inner_two:
        side, along = chip % 2, chip // 2
    else:
        side, along = chip // length, chip % length
    place = along + side * (2 * length - 1 - 2 * along)

    def device_at(position, which):
        return chip_at((position + 2 * chips) % chips) * 2 + which

    sibling = me + 1 - 2 * core
    right = device_at(place + 1, core)
    left = device_at(place - 1, core)

    def send(origin, h, kind, target):
        return pltpu.make_async_remote_copy(
            src_ref=buf.at[origin, h], dst_ref=buf.at[origin, h],
            send_sem=gather_send.at[kind, origin, h], recv_sem=gather_recv.at[origin, h],
            device_id={"blk": target}, device_id_type=MESH)

    def arrived(origin, h):
        send(origin, h, 0, right).wait_recv()

    barrier = pltpu.get_barrier_semaphore()
    pl.semaphore_signal(barrier, inc=1, device_id={"blk": sibling}, device_id_type=MESH)
    for j in range(1, chips):
        pl.semaphore_signal(barrier, inc=1, device_id={"blk": device_at(place + j, core)}, device_id_type=MESH)
    for j in range(1, n_grp):
        pl.semaphore_signal(barrier, inc=1, device_id={"grp": (grp + j) % n_grp}, device_id_type=MESH)
    buf[me] = own_ref[...]
    pl.semaphore_wait(barrier, 1 + (chips - 1) + (n_grp - 1))

    for h in range(2):
        send(me, h, 0, right).start()
        send(me, h, 1, left).start()
        send(me, h, 2, sibling).start()

    near_high, near_low = split(orb_ref[...])
    turned_high, turned_low = split(orb_ref[...].T)
    for k, (near_part, turned_part) in enumerate(
            ((near_high, turned_high), (near_low, turned_low), (near_high, turned_high))):
        near3[:, k * norb:(k + 1) * norb] = near_part
        turned3[:, k * rows:(k + 1) * rows] = turned_part
    acc[...] = jnp.zeros_like(acc)

    def compute(origin):
        for h in range(2):
            high, low = split(buf[origin, h, :piece, :])
            for k, far_part in enumerate((high, high, low)):
                far3[h * piece:(h + 1) * piece, k * norb:(k + 1) * norb] = far_part
                low3[k * width + h * piece:k * width + (h + 1) * piece, :] = far_part
        coords = buf[origin, 0, piece:, :width]

        def rows_of(t, carry):
            here = pl.ds(pl.multiple_of(t * tile, tile), tile)
            gram = dot(near3[here, :], far3[...], ((1,), (1,)))
            squared = jnp.zeros((tile, width), F32)
            for k in range(3):
                spacing = near_ref[here, k:k + 1] - coords[k:k + 1, :]
                squared = squared + spacing * spacing
            high, low = split(gram * lax.rsqrt(squared + 0.0025))
            if width % 128 == 0:
                acc[here, :] += dot(jnp.concatenate([high, low, high], axis=1), low3[...], ((1,), (0,)))
            else:
                top, bottom = low3[:width, :], low3[2 * width:, :]
                acc[here, :] += dot3((high, low), (top, bottom), ((1,), (0,)))
            return carry

        lax.fori_loop(0, rows // tile, rows_of, 0)

    def first(i, carry):
        origin = jnp.where(i == 0, me, sibling)

        @pl.when(i == 1)
        def _():
            arrived(sibling, 0)
            arrived(sibling, 1)

        compute(origin)
        return carry

    lax.fori_loop(0, 2, first, 0)

    full = (chips - 1) // 2

    def service(d, h):
        for kind, sign, target in ((0, -1, right), (1, 1, left)):
            origin = device_at(place + sign * d, core)
            arrived(origin, h)
            if h == kind:
                send(origin, h, kind, target).start()
            else:
                @pl.when(d < full)
                def _():
                    send(origin, h, kind, target).start()
            send(origin, h, 2, sibling).start()

    def pair(d, which, wait):
        def one(i, carry):
            origin = device_at(place + (2 * i - 1) * d, which)
            if wait:
                arrived(origin, 0)
                arrived(origin, 1)
            compute(origin)
            return carry
        lax.fori_loop(0, 2, one, 0)

    def round_of(d, carry):
        service(d, 0)

        @pl.when(d > 1)
        def _():
            pair(d - 1, 1 - core, True)

        service(d, 1)
        pair(d, core, False)
        return carry

    lax.fori_loop(1, full + 1, round_of, 0)
    pair(full, 1 - core, True)
    across = device_at(place + length, core)
    for h in range(2):
        arrived(across, h)
        send(across, h, 2, sibling).start()

    def last(i, carry):
        origin = device_at(place + length, jnp.where(i == 0, core, 1 - core))

        @pl.when(i == 1)
        def _():
            arrived(origin, 0)
            arrived(origin, 1)

        compute(origin)
        return carry

    lax.fori_loop(0, 2, last, 0)

    app_buf[grp] = -weight * acc[...]

    def app_copy(j):
        return pltpu.make_async_remote_copy(
            src_ref=app_buf.at[grp], dst_ref=app_buf.at[grp],
            send_sem=app_send.at[j], recv_sem=app_recv.at[grp],
            device_id={"grp": (grp + j) % n_grp}, device_id_type=MESH)

    def app_in(j):
        other = (grp + j) % n_grp
        return pltpu.make_async_remote_copy(
            src_ref=app_buf.at[other], dst_ref=app_buf.at[other],
            send_sem=app_send.at[j], recv_sem=app_recv.at[other],
            device_id={"grp": other}, device_id_type=MESH)

    high, low = split(acc[...])
    scaled3 = jnp.concatenate([high, high, low], axis=0)
    blocks = [(i, j) for i in range(norb // BASE) for j in range(i + 1)]
    for i in range(norb // BASE):
        made = dot(turned3[i * BASE:(i + 1) * BASE, :], scaled3[:, :(i + 1) * BASE], ((1,), (0,)))
        made = made * (weight * weight)
        for j in range(i + 1):
            side_of, index = divmod(blocks.index((i, j)), len(blocks) // 2)
            part[side_of, index * BASE:(index + 1) * BASE, :] = made[:, j * BASE:(j + 1) * BASE]
    to_sibling = pltpu.make_async_remote_copy(
        src_ref=part.at[1 - core], dst_ref=half_buf, send_sem=half_sem.at[0], recv_sem=half_sem.at[1],
        device_id={"blk": sibling}, device_id_type=MESH)
    to_sibling.start()
    for j in range(1, n_grp):
        app_copy(j).start()
    to_sibling.wait_recv()
    red[...] = (part[core] + half_buf[...]).reshape(red.shape)

    def rs_copy(j):
        to = (place + j) % chips
        return pltpu.make_async_remote_copy(
            src_ref=red.at[to], dst_ref=rs_buf.at[j], send_sem=rs_send.at[j], recv_sem=rs_recv.at[j],
            device_id={"blk": device_at(to, core)}, device_id_type=MESH)

    for j in range(1, chips):
        rs_copy(j).start()
    total = red[place]
    for j in range(1, chips):
        rs_copy(j).wait_recv()
        total = total + rs_buf[j]
    grp_buf[grp] = total

    def grp_copy(j):
        return pltpu.make_async_remote_copy(
            src_ref=grp_buf.at[grp], dst_ref=grp_buf.at[grp],
            send_sem=grp_send.at[j], recv_sem=grp_recv.at[grp],
            device_id={"grp": (grp + j) % n_grp}, device_id_type=MESH)

    def grp_in(j):
        other = (grp + j) % n_grp
        return pltpu.make_async_remote_copy(
            src_ref=grp_buf.at[other], dst_ref=grp_buf.at[other],
            send_sem=grp_send.at[j], recv_sem=grp_recv.at[other],
            device_id={"grp": other}, device_id_type=MESH)

    for j in range(1, n_grp):
        grp_copy(j).start()
    for j in range(1, n_grp):
        grp_in(j).wait_recv()
    total = grp_buf[0]
    for j in range(1, n_grp):
        total = total + grp_buf[j]
    mine = core * chips + place
    corr_buf[mine] = total

    def ag_copy(block, sem, target):
        return pltpu.make_async_remote_copy(
            src_ref=corr_buf.at[block], dst_ref=corr_buf.at[block],
            send_sem=sem, recv_sem=ag_recv.at[block],
            device_id={"blk": target}, device_id_type=MESH)

    for j in range(1, chips):
        ag_copy(mine, ag_send.at[j], device_at(place + j, core)).start()
    ag_copy(mine, ag_sib.at[0], sibling).start()
    for j in range(1, chips):
        block = core * chips + (place + chips - j) % chips
        ag_copy(block, ag_sib.at[j], sibling).wait_recv()
        ag_copy(block, ag_sib.at[j], sibling).start()
    for j in range(chips):
        block = (1 - core) * chips + (place + chips - j) % chips
        ag_copy(block, ag_sib.at[j], sibling).wait_recv()
    corr_ref[...] = corr_buf[...]

    for j in range(1, n_grp):
        app_in(j).wait_recv()
    whole = app_buf[0]
    for j in range(1, n_grp):
        whole = whole + app_buf[j]
    applied_ref[...] = whole

    def sent(d, carry):
        for kind, sign, target in ((0, -1, right), (1, 1, left)):
            origin = device_at(place + sign * d, core)
            for h in range(2):
                if h == kind:
                    send(origin, h, kind, target).wait_send()
                else:
                    @pl.when(d < full)
                    def _():
                        send(origin, h, kind, target).wait_send()
                send(origin, h, 2, sibling).wait_send()
        return carry

    lax.fori_loop(1, full + 1, sent, 0)
    for h in range(2):
        send(me, h, 0, right).wait_send()
        send(me, h, 1, left).wait_send()
        send(me, h, 2, sibling).wait_send()
        send(across, h, 2, sibling).wait_send()
    to_sibling.wait_send()
    for j in range(1, chips):
        rs_copy(j).wait_send()
        ag_copy(mine, ag_send.at[j], device_at(place + j, core)).wait_send()
    for j in range(chips):
        block = core * chips + (place + chips - j) % chips
        ag_copy(block, ag_sib.at[j], sibling).wait_send()
    for j in range(1, n_grp):
        app_copy(j).wait_send()
        grp_copy(j).wait_send()


def split3(value):
    high = value.astype(BF16).astype(F32)
    rest = value - high
    middle = rest.astype(BF16).astype(F32)
    return high, middle, rest - middle


def diagonal_inverse(work):
    size = work.shape[0]
    sub = lax.broadcasted_iota(jnp.int32, (8, size), 0)
    lane = lax.broadcasted_iota(jnp.int32, (8, size), 1)

    def eliminate(top, both):
        count = 2 if both else 1
        left = [work[top + 8 * r:top + 8 * r + 8, :size] for r in range(count)]
        right = [work[top + 8 * r:top + 8 * r + 8, size:] for r in range(count)]
        cols = [[jnp.broadcast_to(left[r][:, top + j:top + j + 1], (8, size)) for j in range(8)] for r in range(count)]
        scale = jnp.ones((8, size), F32)
        for j in range(8):
            root = lax.rsqrt(jnp.broadcast_to(cols[0][j][j:j + 1, :], (8, size)))
            scale = jnp.where(sub == j, root, scale)
            inverse = root * root
            left_row, right_row = left[0][j:j + 1, :], right[0][j:j + 1, :]
            col_rows = [cols[0][m][j:j + 1, :] for m in range(8)]
            for r in range(count):
                factor = cols[r][j] * inverse
                if r == 0:
                    factor = jnp.where(sub > j, factor, 0.0)
                for m in range(j + 1, 8):
                    cols[r][m] = cols[r][m] - factor * col_rows[m]
                left[r] = left[r] - factor * left_row
                right[r] = right[r] - factor * right_row
        pivots_left, pivots_right = left[0] * scale, right[0] * scale
        work[top:top + 8, size:] = pivots_right
        if both:
            work[top + 8:top + 16, :size] = left[1]
            work[top + 8:top + 16, size:] = right[1]
        rest = top + 16
        if rest < size:
            below = jnp.where(lane >= rest, pivots_left, 0.0)
            bh, bm, bl = split3(below)
            ah, am, al = split3(jnp.concatenate([pivots_left, pivots_right], axis=1))
            near = jnp.concatenate([bh, bh, bm, bh, bl, bm], axis=0).astype(BF16)
            far = jnp.concatenate([ah, am, ah, al, ah, am], axis=0).astype(BF16)
            update = dot(near, far, ((0,), (0,)))
            work[rest:, :] -= update[rest:, :]

    for step in range(size // 8):
        eliminate(8 * step, 8 * step + 8 < size)


def solve_kernel(corr_ref, applied_ref, out_ref, a, work):
    norb = applied_ref.shape[1]
    rows = applied_ref.shape[0]
    base = BASE
    index = 0
    for i in range(norb // base):
        for j in range(i + 1):
            a[i * base:(i + 1) * base, j * base:(j + 1) * base] = corr_ref[index * base:(index + 1) * base, :]
            index += 1
    a[norb:, :] = applied_ref[...]
    eye = (lax.broadcasted_iota(jnp.int32, (base, base), 0)
           == lax.broadcasted_iota(jnp.int32, (base, base), 1)).astype(F32)
    for b in range(norb // base):
        here = slice(b * base, (b + 1) * base)
        work[:, :base] = a[here, here]
        work[:, base:] = eye
        diagonal_inverse(work)
        inverse = work[:, base:]
        below = slice((b + 1) * base, norb + rows)
        a[below, here] = lax.dot_general(
            a[below, here], inverse, (((1,), (1,)), ((), ())), precision=HIGHEST, preferred_element_type=F32)
        for j in range(b + 1, norb // base):
            there = slice(j * base, (j + 1) * base)
            low = slice(j * base, norb + rows)
            a[low, there] -= lax.dot_general(
                a[low, here], a[there, here], (((1,), (1,)), ((), ())),
                precision=HIGHEST, preferred_element_type=F32)
    out_ref[...] = a[norb:, :]


def solution(mesh):
    n_blk, n_grp = mesh.shape["blk"], mesh.shape["grp"]
    inner_two = two_wide(mesh)
    chips = n_blk // 2

    def shards(orbitals, points):
        rows, norb = orbitals.shape
        weight = 1.0 / (rows * n_blk)
        width = rows // n_grp
        piece = width // 2
        start = lax.axis_index("grp") * width
        far_rows = lax.dynamic_slice_in_dim(orbitals, start, width, 0).reshape(2, piece, norb)
        far_coords = lax.dynamic_slice_in_dim(points, start, width, 1)
        far_coords = jnp.pad(far_coords, ((0, PAD - 3), (0, norb - width)))
        own = jnp.concatenate([far_rows, jnp.broadcast_to(far_coords, (2, PAD, norb))], axis=1)
        packed = norb * (norb // BASE + 1) // 2
        share = packed // n_blk
        vmem = pl.BlockSpec(memory_space=pltpu.VMEM)
        dma = pltpu.SemaphoreType.DMA
        applied, corr = pl.pallas_call(
            functools.partial(apply_kernel, (n_blk, n_grp, inner_two, weight, min(256, rows))),
            out_shape=[jax.ShapeDtypeStruct((rows, norb), F32), jax.ShapeDtypeStruct((n_blk, share, BASE), F32)],
            in_specs=[vmem] * 3,
            out_specs=[vmem] * 2,
            scratch_shapes=[
                pltpu.VMEM((n_blk, 2, piece + PAD, norb), F32),
                pltpu.VMEM((rows, 3 * norb), BF16),
                pltpu.VMEM((norb, 3 * rows), BF16),
                pltpu.VMEM((width, 3 * norb), BF16),
                pltpu.VMEM((3 * width, norb), BF16),
                pltpu.VMEM((rows, norb), F32),
                pltpu.VMEM((2, packed // 2, BASE), F32),
                pltpu.VMEM((packed // 2, BASE), F32),
                pltpu.VMEM((chips, share, BASE), F32),
                pltpu.VMEM((chips, share, BASE), F32),
                pltpu.VMEM((n_grp, share, BASE), F32),
                pltpu.VMEM((n_blk, share, BASE), F32),
                pltpu.VMEM((n_grp, rows, norb), F32),
                dma((n_blk, 2)), dma((3, n_blk, 2)), dma((2,)), dma((chips,)), dma((chips,)),
                dma((n_grp,)), dma((n_grp,)), dma((n_blk,)), dma((chips,)), dma((chips,)),
                dma((n_grp,)), dma((n_grp,)),
            ],
            compiler_params=pltpu.CompilerParams(
                collective_id=0, has_side_effects=True, vmem_limit_bytes=48 << 20),
            name="apply_and_correlate",
        )(orbitals, own, points.T)
        return pl.pallas_call(
            solve_kernel,
            out_shape=jax.ShapeDtypeStruct((rows, norb), F32),
            in_specs=[vmem] * 2,
            out_specs=vmem,
            scratch_shapes=[pltpu.VMEM((norb + rows, norb), F32), pltpu.VMEM((128, 256), F32)],
            compiler_params=pltpu.CompilerParams(vmem_limit_bytes=32 << 20),
            name="factor_and_solve",
        )(corr.reshape(packed, BASE), applied)

    return jax.shard_map(
        shards,
        mesh=mesh,
        in_specs=(P("blk", None), P(None, "blk")),
        out_specs=P("blk", None),
        check_vma=False,
    )
```

```python
import functools

import jax
import jax.numpy as jnp
from jax import lax
from jax.experimental import pallas as pl
from jax.experimental.pallas import tpu as pltpu
from jax.sharding import PartitionSpec as P

MESH = pl.DeviceIdType.MESH
F32 = jnp.float32
BF16 = jnp.bfloat16
HIGHEST = lax.Precision.HIGHEST
PAD = 8
BASE = 128
PIECES = 4


def two_wide(mesh):
    devices = mesh.devices.reshape(mesh.shape["blk"], mesh.shape["grp"])
    if devices.shape[0] < 6:
        return True
    near = getattr(devices[0, 0], "coords", None)
    far = getattr(devices[4, 0], "coords", None)
    if near is None or far is None:
        return True
    return sum(abs(a - b) for a, b in zip(near, far)) == 1


def split(value):
    high = value.astype(BF16)
    return high, (value - high.astype(F32)).astype(BF16)


def dot(a, b, dims):
    return lax.dot_general(a, b, (dims, ((), ())), preferred_element_type=F32)


def dot3(a, b, dims):
    return dot(a[0], b[0], dims) + (dot(a[1], b[0], dims) + dot(a[0], b[1], dims))


def apply_kernel(
    sizes, orb_ref, own_ref, near_ref, applied_ref, corr_ref,
    buf, near3, turned3, far3, low3, acc, part, half_buf, red, rs_buf, grp_buf, corr_buf, app_buf,
    gather_recv, gather_send, half_sem, rs_send, rs_recv, grp_send, grp_recv,
    ag_recv, ag_send, ag_sib, app_send, app_recv,
):
    n_blk, n_grp, inner_two, weight, tile = sizes
    chips = n_blk // 2
    length = chips // 2
    rows, norb = orb_ref.shape
    width = own_ref.shape[0] - PAD
    piece = width // PIECES
    me = lax.axis_index("blk")
    grp = lax.axis_index("grp")
    core = me % 2
    chip = me // 2

    def chip_at(position):
        side = position // length
        along = side * (2 * length - 1 - 2 * position) + position
        return along * 2 + side if inner_two else side * length + along

    if inner_two:
        side, along = chip % 2, chip // 2
    else:
        side, along = chip // length, chip % length
    place = along + side * (2 * length - 1 - 2 * along)

    def device_at(position, which):
        return chip_at((position + 2 * chips) % chips) * 2 + which

    sibling = me + 1 - 2 * core
    right = device_at(place + 1, core)
    left = device_at(place - 1, core)

    def send(origin, h, kind, target):
        place_of = pl.ds(0, PAD + piece) if h == 0 else pl.ds(PAD + h * piece, piece)
        return pltpu.make_async_remote_copy(
            src_ref=buf.at[origin, place_of], dst_ref=buf.at[origin, place_of],
            send_sem=gather_send.at[kind, origin, h], recv_sem=gather_recv.at[origin, h],
            device_id={"blk": target}, device_id_type=MESH)

    def arrived(origin, h):
        send(origin, h, 0, right).wait_recv()

    barrier = pltpu.get_barrier_semaphore()
    pl.semaphore_signal(barrier, inc=1, device_id={"blk": sibling}, device_id_type=MESH)
    for j in range(1, chips):
        pl.semaphore_signal(barrier, inc=1, device_id={"blk": device_at(place + j, core)}, device_id_type=MESH)
    for j in range(1, n_grp):
        pl.semaphore_signal(barrier, inc=1, device_id={"grp": (grp + j) % n_grp}, device_id_type=MESH)
    buf[me] = own_ref[...]
    pl.semaphore_wait(barrier, 1 + (chips - 1) + (n_grp - 1))

    for h in range(PIECES):
        send(me, h, 0, right).start()
        send(me, h, 1, left).start()
        send(me, h, 2, sibling).start()

    near_high, near_low = split(orb_ref[...])
    turned_high, turned_low = split(orb_ref[...].T)
    for k, (near_part, turned_part) in enumerate(
            ((near_high, turned_high), (near_low, turned_low), (near_high, turned_high))):
        near3[:, k * norb:(k + 1) * norb] = near_part
        turned3[:, k * rows:(k + 1) * rows] = turned_part
    acc[...] = jnp.zeros_like(acc)

    def compute(origin):
        high, low = split(buf[origin, PAD:, :])
        for k, far_part in enumerate((high, high, low)):
            far3[:, k * norb:(k + 1) * norb] = far_part
            low3[k * width:(k + 1) * width, :] = far_part
        coords = buf[origin, :PAD, :width]

        def rows_of(t, carry):
            here = pl.ds(pl.multiple_of(t * tile, tile), tile)
            gram = dot(near3[here, :], far3[...], ((1,), (1,)))
            squared = jnp.zeros((tile, width), F32)
            for k in range(3):
                spacing = near_ref[here, k:k + 1] - coords[k:k + 1, :]
                squared = squared + spacing * spacing
            high, low = split(gram * lax.rsqrt(squared + 0.0025))
            if width % 128 == 0:
                acc[here, :] += dot(jnp.concatenate([high, low, high], axis=1), low3[...], ((1,), (0,)))
            else:
                top, bottom = low3[:width, :], low3[2 * width:, :]
                acc[here, :] += dot3((high, low), (top, bottom), ((1,), (0,)))
            return carry

        lax.fori_loop(0, rows // tile, rows_of, 0)

    full = (chips - 1) // 2

    def onward(d, h, kind, act):
        if (h < PIECES // 2) == (kind == 0):
            act()
        else:
            pl.when(d < full)(act)

    def service(d, h):
        for kind, sign, target in ((0, -1, right), (1, 1, left)):
            origin = device_at(place + sign * d, core)
            arrived(origin, h)
            onward(d, h, kind, lambda: send(origin, h, kind, target).start())
            send(origin, h, 2, sibling).start()

    def block_of(d, k):
        which = core if k < 2 else 1 - core
        origin = device_at(place + (2 * (k % 2) - 1) * d, which)

        def work():
            if k >= 2:
                for h in range(PIECES):
                    arrived(origin, h)
            compute(origin)

        if k % 2:
            pl.when(d > 0)(work)
        else:
            work()

    def round_of(d, carry):
        for k in range(4):
            service(d, k)
            block_of(d - 1, k)
        return carry

    lax.fori_loop(1, full + 1, round_of, 0)
    across = device_at(place + length, core)

    def last(k, carry):
        which = jnp.where(k < 2, core, 1 - core)
        origin = device_at(place + (2 * (k % 2) - 1) * full, which)

        @pl.when(k >= 2)
        def _():
            for h in range(PIECES):
                arrived(origin, h)

        for h in range(PIECES):
            @pl.when(k == h)
            def _():
                arrived(across, h)
                send(across, h, 2, sibling).start()

        compute(origin)
        return carry

    lax.fori_loop(0, 4, last, 0)

    def final(i, carry):
        origin = device_at(place + length, jnp.where(i == 0, core, 1 - core))

        @pl.when(i == 1)
        def _():
            for h in range(PIECES):
                arrived(origin, h)

        compute(origin)
        return carry

    lax.fori_loop(0, 2, final, 0)

    app_buf[grp] = -weight * acc[...]

    def app_copy(j):
        return pltpu.make_async_remote_copy(
            src_ref=app_buf.at[grp], dst_ref=app_buf.at[grp],
            send_sem=app_send.at[j], recv_sem=app_recv.at[grp],
            device_id={"grp": (grp + j) % n_grp}, device_id_type=MESH)

    def app_in(j):
        other = (grp + j) % n_grp
        return pltpu.make_async_remote_copy(
            src_ref=app_buf.at[other], dst_ref=app_buf.at[other],
            send_sem=app_send.at[j], recv_sem=app_recv.at[other],
            device_id={"grp": other}, device_id_type=MESH)

    high, low = split(acc[...])
    scaled3 = jnp.concatenate([high, high, low], axis=0)
    blocks = [(i, j) for i in range(norb // BASE) for j in range(i + 1)]
    for i in range(norb // BASE):
        made = dot(turned3[i * BASE:(i + 1) * BASE, :], scaled3[:, :(i + 1) * BASE], ((1,), (0,)))
        made = made * (weight * weight)
        for j in range(i + 1):
            side_of, index = divmod(blocks.index((i, j)), len(blocks) // 2)
            part[side_of, index * BASE:(index + 1) * BASE, :] = made[:, j * BASE:(j + 1) * BASE]
    to_sibling = pltpu.make_async_remote_copy(
        src_ref=part.at[1 - core], dst_ref=half_buf, send_sem=half_sem.at[0], recv_sem=half_sem.at[1],
        device_id={"blk": sibling}, device_id_type=MESH)
    to_sibling.start()
    for j in range(1, n_grp):
        app_copy(j).start()
    to_sibling.wait_recv()
    red[...] = (part[core] + half_buf[...]).reshape(red.shape)

    def rs_copy(j):
        to = (place + j) % chips
        return pltpu.make_async_remote_copy(
            src_ref=red.at[to], dst_ref=rs_buf.at[j], send_sem=rs_send.at[j], recv_sem=rs_recv.at[j],
            device_id={"blk": device_at(to, core)}, device_id_type=MESH)

    for j in range(1, chips):
        rs_copy(j).start()
    total = red[place]
    for j in range(1, chips):
        rs_copy(j).wait_recv()
        total = total + rs_buf[j]
    grp_buf[grp] = total

    def grp_copy(j):
        return pltpu.make_async_remote_copy(
            src_ref=grp_buf.at[grp], dst_ref=grp_buf.at[grp],
            send_sem=grp_send.at[j], recv_sem=grp_recv.at[grp],
            device_id={"grp": (grp + j) % n_grp}, device_id_type=MESH)

    def grp_in(j):
        other = (grp + j) % n_grp
        return pltpu.make_async_remote_copy(
            src_ref=grp_buf.at[other], dst_ref=grp_buf.at[other],
            send_sem=grp_send.at[j], recv_sem=grp_recv.at[other],
            device_id={"grp": other}, device_id_type=MESH)

    for j in range(1, n_grp):
        grp_copy(j).start()
    for j in range(1, n_grp):
        grp_in(j).wait_recv()
    total = grp_buf[0]
    for j in range(1, n_grp):
        total = total + grp_buf[j]
    mine = core * chips + place
    corr_buf[mine] = total

    def ag_copy(block, sem, target):
        return pltpu.make_async_remote_copy(
            src_ref=corr_buf.at[block], dst_ref=corr_buf.at[block],
            send_sem=sem, recv_sem=ag_recv.at[block],
            device_id={"blk": target}, device_id_type=MESH)

    for j in range(1, chips):
        ag_copy(mine, ag_send.at[j], device_at(place + j, core)).start()
    ag_copy(mine, ag_sib.at[0], sibling).start()
    for j in range(1, chips):
        block = core * chips + (place + chips - j) % chips
        ag_copy(block, ag_sib.at[j], sibling).wait_recv()
        ag_copy(block, ag_sib.at[j], sibling).start()
    for j in range(chips):
        block = (1 - core) * chips + (place + chips - j) % chips
        ag_copy(block, ag_sib.at[j], sibling).wait_recv()
    corr_ref[...] = corr_buf[...]

    for j in range(1, n_grp):
        app_in(j).wait_recv()
    whole = app_buf[0]
    for j in range(1, n_grp):
        whole = whole + app_buf[j]
    applied_ref[...] = whole

    def sent(d, carry):
        for kind, sign, target in ((0, -1, right), (1, 1, left)):
            origin = device_at(place + sign * d, core)
            for h in range(PIECES):
                onward(d, h, kind, lambda: send(origin, h, kind, target).wait_send())
                send(origin, h, 2, sibling).wait_send()
        return carry

    lax.fori_loop(1, full + 1, sent, 0)
    for h in range(PIECES):
        send(me, h, 0, right).wait_send()
        send(me, h, 1, left).wait_send()
        send(me, h, 2, sibling).wait_send()
        send(across, h, 2, sibling).wait_send()
    to_sibling.wait_send()
    for j in range(1, chips):
        rs_copy(j).wait_send()
        ag_copy(mine, ag_send.at[j], device_at(place + j, core)).wait_send()
    for j in range(chips):
        block = core * chips + (place + chips - j) % chips
        ag_copy(block, ag_sib.at[j], sibling).wait_send()
    for j in range(1, n_grp):
        app_copy(j).wait_send()
        grp_copy(j).wait_send()


def split3(value):
    high = value.astype(BF16).astype(F32)
    rest = value - high
    middle = rest.astype(BF16).astype(F32)
    return high, middle, rest - middle


def diagonal_inverse(work):
    size = work.shape[0]
    sub = lax.broadcasted_iota(jnp.int32, (8, size), 0)
    lane = lax.broadcasted_iota(jnp.int32, (8, size), 1)

    def eliminate(top, both):
        count = 2 if both else 1
        left = [work[top + 8 * r:top + 8 * r + 8, :size] for r in range(count)]
        right = [work[top + 8 * r:top + 8 * r + 8, size:] for r in range(count)]
        cols = [[jnp.broadcast_to(left[r][:, top + j:top + j + 1], (8, size)) for j in range(8)] for r in range(count)]
        scale = jnp.ones((8, size), F32)
        for j in range(8):
            root = lax.rsqrt(jnp.broadcast_to(cols[0][j][j:j + 1, :], (8, size)))
            scale = jnp.where(sub == j, root, scale)
            inverse = root * root
            left_row, right_row = left[0][j:j + 1, :], right[0][j:j + 1, :]
            col_rows = [cols[0][m][j:j + 1, :] for m in range(8)]
            for r in range(count):
                factor = cols[r][j] * inverse
                if r == 0:
                    factor = jnp.where(sub > j, factor, 0.0)
                for m in range(j + 1, 8):
                    cols[r][m] = cols[r][m] - factor * col_rows[m]
                left[r] = left[r] - factor * left_row
                right[r] = right[r] - factor * right_row
        pivots_left, pivots_right = left[0] * scale, right[0] * scale
        work[top:top + 8, size:] = pivots_right
        if both:
            work[top + 8:top + 16, :size] = left[1]
            work[top + 8:top + 16, size:] = right[1]
        rest = top + 16
        if rest < size:
            below = jnp.where(lane >= rest, pivots_left, 0.0)
            bh, bm, bl = split3(below)
            ah, am, al = split3(jnp.concatenate([pivots_left, pivots_right], axis=1))
            near = jnp.concatenate([bh, bh, bm, bh, bl, bm], axis=0).astype(BF16)
            far = jnp.concatenate([ah, am, ah, al, ah, am], axis=0).astype(BF16)
            update = dot(near, far, ((0,), (0,)))
            work[rest:, :] -= update[rest:, :]

    for step in range(size // 8):
        eliminate(8 * step, 8 * step + 8 < size)


def solve_kernel(corr_ref, applied_ref, out_ref, a, work):
    norb = applied_ref.shape[1]
    rows = applied_ref.shape[0]
    base = BASE
    index = 0
    for i in range(norb // base):
        for j in range(i + 1):
            a[i * base:(i + 1) * base, j * base:(j + 1) * base] = corr_ref[index * base:(index + 1) * base, :]
            index += 1
    a[norb:, :] = applied_ref[...]
    eye = (lax.broadcasted_iota(jnp.int32, (base, base), 0)
           == lax.broadcasted_iota(jnp.int32, (base, base), 1)).astype(F32)
    for b in range(norb // base):
        here = slice(b * base, (b + 1) * base)
        work[:, :base] = a[here, here]
        work[:, base:] = eye
        diagonal_inverse(work)
        inverse = work[:, base:]
        below = slice((b + 1) * base, norb + rows)
        a[below, here] = lax.dot_general(
            a[below, here], inverse, (((1,), (1,)), ((), ())), precision=HIGHEST, preferred_element_type=F32)
        for j in range(b + 1, norb // base):
            there = slice(j * base, (j + 1) * base)
            low = slice(j * base, norb + rows)
            a[low, there] -= lax.dot_general(
                a[low, here], a[there, here], (((1,), (1,)), ((), ())),
                precision=HIGHEST, preferred_element_type=F32)
    out_ref[...] = a[norb:, :]


def solution(mesh):
    n_blk, n_grp = mesh.shape["blk"], mesh.shape["grp"]
    inner_two = two_wide(mesh)
    chips = n_blk // 2

    def shards(orbitals, points):
        rows, norb = orbitals.shape
        weight = 1.0 / (rows * n_blk)
        width = rows // n_grp
        start = lax.axis_index("grp") * width
        far_rows = lax.dynamic_slice_in_dim(orbitals, start, width, 0)
        far_coords = lax.dynamic_slice_in_dim(points, start, width, 1)
        far_coords = jnp.pad(far_coords, ((0, PAD - 3), (0, norb - width)))
        own = jnp.concatenate([far_coords, far_rows], axis=0)
        packed = norb * (norb // BASE + 1) // 2
        share = packed // n_blk
        vmem = pl.BlockSpec(memory_space=pltpu.VMEM)
        dma = pltpu.SemaphoreType.DMA
        applied, corr = pl.pallas_call(
            functools.partial(apply_kernel, (n_blk, n_grp, inner_two, weight, min(512, rows))),
            out_shape=[jax.ShapeDtypeStruct((rows, norb), F32), jax.ShapeDtypeStruct((n_blk, share, BASE), F32)],
            in_specs=[vmem] * 3,
            out_specs=[vmem] * 2,
            scratch_shapes=[
                pltpu.VMEM((n_blk, PAD + width, norb), F32),
                pltpu.VMEM((rows, 3 * norb), BF16),
                pltpu.VMEM((norb, 3 * rows), BF16),
                pltpu.VMEM((width, 3 * norb), BF16),
                pltpu.VMEM((3 * width, norb), BF16),
                pltpu.VMEM((rows, norb), F32),
                pltpu.VMEM((2, packed // 2, BASE), F32),
                pltpu.VMEM((packed // 2, BASE), F32),
                pltpu.VMEM((chips, share, BASE), F32),
                pltpu.VMEM((chips, share, BASE), F32),
                pltpu.VMEM((n_grp, share, BASE), F32),
                pltpu.VMEM((n_blk, share, BASE), F32),
                pltpu.VMEM((n_grp, rows, norb), F32),
                dma((n_blk, PIECES)), dma((3, n_blk, PIECES)), dma((2,)), dma((chips,)), dma((chips,)),
                dma((n_grp,)), dma((n_grp,)), dma((n_blk,)), dma((chips,)), dma((chips,)),
                dma((n_grp,)), dma((n_grp,)),
            ],
            compiler_params=pltpu.CompilerParams(
                collective_id=0, has_side_effects=True, vmem_limit_bytes=48 << 20),
            name="apply_and_correlate",
        )(orbitals, own, points.T)
        return pl.pallas_call(
            solve_kernel,
            out_shape=jax.ShapeDtypeStruct((rows, norb), F32),
            in_specs=[vmem] * 2,
            out_specs=vmem,
            scratch_shapes=[pltpu.VMEM((norb + rows, norb), F32), pltpu.VMEM((128, 256), F32)],
            compiler_params=pltpu.CompilerParams(vmem_limit_bytes=32 << 20),
            name="factor_and_solve",
        )(corr.reshape(packed, BASE), applied)

    return jax.shard_map(
        shards,
        mesh=mesh,
        in_specs=(P("blk", None), P(None, "blk")),
        out_specs=P("blk", None),
        check_vma=False,
    )
```

```python
import functools

import jax
import jax.numpy as jnp
from jax import lax
from jax.experimental import pallas as pl
from jax.experimental.pallas import tpu as pltpu
from jax.sharding import PartitionSpec as P

MESH = pl.DeviceIdType.MESH
F32 = jnp.float32
BF16 = jnp.bfloat16
HIGHEST = lax.Precision.HIGHEST
PAD = 8
BASE = 128
PIECES = 4


def two_wide(mesh):
    devices = mesh.devices.reshape(mesh.shape["blk"], mesh.shape["grp"])
    if devices.shape[0] < 6:
        return True
    near = getattr(devices[0, 0], "coords", None)
    far = getattr(devices[4, 0], "coords", None)
    if near is None or far is None:
        return True
    return sum(abs(a - b) for a, b in zip(near, far)) == 1


def split(value):
    high = value.astype(BF16)
    return high, (value - high.astype(F32)).astype(BF16)


def dot(a, b, dims):
    return lax.dot_general(a, b, (dims, ((), ())), preferred_element_type=F32)


def dot3(a, b, dims):
    return dot(a[0], b[0], dims) + (dot(a[1], b[0], dims) + dot(a[0], b[1], dims))


def apply_kernel(
    sizes, orb_ref, own_ref, near_ref, out_ref,
    buf, near3, turned3, far3, low3, acc, part, half_buf, red, rs_buf, grp_buf, corr_buf, app_buf,
    gather_recv, gather_send, half_sem, rs_send, rs_recv, grp_send, grp_recv,
    ag_recv, ag_send, ag_sib, app_send, app_recv, a, inverses, work,
):
    n_blk, n_grp, inner_two, weight, tile = sizes
    chips = n_blk // 2
    length = chips // 2
    rows, norb = orb_ref.shape
    width = own_ref.shape[0] - PAD
    piece = width // PIECES
    me = lax.axis_index("blk")
    grp = lax.axis_index("grp")
    core = me % 2
    chip = me // 2

    def chip_at(position):
        side = position // length
        along = side * (2 * length - 1 - 2 * position) + position
        return along * 2 + side if inner_two else side * length + along

    if inner_two:
        side, along = chip % 2, chip // 2
    else:
        side, along = chip // length, chip % length
    place = along + side * (2 * length - 1 - 2 * along)

    def device_at(position, which):
        return chip_at((position + 2 * chips) % chips) * 2 + which

    sibling = me + 1 - 2 * core
    right = device_at(place + 1, core)
    left = device_at(place - 1, core)

    def send(origin, h, kind, target):
        place_of = pl.ds(0, PAD + piece) if h == 0 else pl.ds(PAD + h * piece, piece)
        return pltpu.make_async_remote_copy(
            src_ref=buf.at[origin, place_of], dst_ref=buf.at[origin, place_of],
            send_sem=gather_send.at[kind, origin, h], recv_sem=gather_recv.at[origin, h],
            device_id={"blk": target}, device_id_type=MESH)

    def arrived(origin, h):
        send(origin, h, 0, right).wait_recv()

    barrier = pltpu.get_barrier_semaphore()
    pl.semaphore_signal(barrier, inc=1, device_id={"blk": sibling}, device_id_type=MESH)
    for j in range(1, chips):
        pl.semaphore_signal(barrier, inc=1, device_id={"blk": device_at(place + j, core)}, device_id_type=MESH)
    for j in range(1, n_grp):
        pl.semaphore_signal(barrier, inc=1, device_id={"grp": (grp + j) % n_grp}, device_id_type=MESH)
    buf[me] = own_ref[...]
    pl.semaphore_wait(barrier, 1 + (chips - 1) + (n_grp - 1))

    for h in range(PIECES):
        send(me, h, 0, right).start()
        send(me, h, 1, left).start()
        send(me, h, 2, sibling).start()

    near_high, near_low = split(orb_ref[...])
    turned_high, turned_low = split(orb_ref[...].T)
    for k, (near_part, turned_part) in enumerate(
            ((near_high, turned_high), (near_low, turned_low), (near_high, turned_high))):
        near3[:, k * norb:(k + 1) * norb] = near_part
        turned3[:, k * rows:(k + 1) * rows] = turned_part
    acc[...] = jnp.zeros_like(acc)

    def compute(origin):
        high, low = split(buf[origin, PAD:, :])
        for k, far_part in enumerate((high, high, low)):
            far3[:, k * norb:(k + 1) * norb] = far_part
            low3[k * width:(k + 1) * width, :] = far_part
        coords = buf[origin, :PAD, :width]

        def rows_of(t, carry):
            here = pl.ds(pl.multiple_of(t * tile, tile), tile)
            gram = dot(near3[here, :], far3[...], ((1,), (1,)))
            squared = jnp.zeros((tile, width), F32)
            for k in range(3):
                spacing = near_ref[here, k:k + 1] - coords[k:k + 1, :]
                squared = squared + spacing * spacing
            high, low = split(gram * lax.rsqrt(squared + 0.0025))
            if width % 128 == 0:
                acc[here, :] += dot(jnp.concatenate([high, low, high], axis=1), low3[...], ((1,), (0,)))
            else:
                top, bottom = low3[:width, :], low3[2 * width:, :]
                acc[here, :] += dot3((high, low), (top, bottom), ((1,), (0,)))
            return carry

        lax.fori_loop(0, rows // tile, rows_of, 0)

    full = (chips - 1) // 2

    def onward(d, h, kind, act):
        if (h < PIECES // 2) == (kind == 0):
            act()
        else:
            pl.when(d < full)(act)

    def service(d, h):
        for kind, sign, target in ((0, -1, right), (1, 1, left)):
            origin = device_at(place + sign * d, core)
            arrived(origin, h)
            onward(d, h, kind, lambda: send(origin, h, kind, target).start())
            send(origin, h, 2, sibling).start()

    def block_of(d, k):
        which = core if k < 2 else 1 - core
        origin = device_at(place + (2 * (k % 2) - 1) * d, which)

        def work():
            if k >= 2:
                for h in range(PIECES):
                    arrived(origin, h)
            compute(origin)

        if k % 2:
            pl.when(d > 0)(work)
        else:
            work()

    def round_of(d, carry):
        for k in range(4):
            service(d, k)
            block_of(d - 1, k)
        return carry

    lax.fori_loop(1, full + 1, round_of, 0)
    across = device_at(place + length, core)

    def last(k, carry):
        which = jnp.where(k < 2, core, 1 - core)
        origin = device_at(place + (2 * (k % 2) - 1) * full, which)

        @pl.when(k >= 2)
        def _():
            for h in range(PIECES):
                arrived(origin, h)

        for h in range(PIECES):
            @pl.when(k == h)
            def _():
                arrived(across, h)
                send(across, h, 2, sibling).start()

        compute(origin)
        return carry

    lax.fori_loop(0, 4, last, 0)

    def final(i, carry):
        origin = device_at(place + length, jnp.where(i == 0, core, 1 - core))

        @pl.when(i == 1)
        def _():
            for h in range(PIECES):
                arrived(origin, h)

        compute(origin)
        return carry

    lax.fori_loop(0, 2, final, 0)

    app_buf[grp] = -weight * acc[...]

    quarter = rows // PIECES

    def app_copy(j, h):
        lines = pl.ds(h * quarter, quarter)
        return pltpu.make_async_remote_copy(
            src_ref=app_buf.at[grp, lines], dst_ref=app_buf.at[grp, lines],
            send_sem=app_send.at[j, h], recv_sem=app_recv.at[grp, h],
            device_id={"grp": (grp + j) % n_grp}, device_id_type=MESH)

    def app_in(j, h):
        other = (grp + j) % n_grp
        lines = pl.ds(h * quarter, quarter)
        return pltpu.make_async_remote_copy(
            src_ref=app_buf.at[other, lines], dst_ref=app_buf.at[other, lines],
            send_sem=app_send.at[j, h], recv_sem=app_recv.at[other, h],
            device_id={"grp": other}, device_id_type=MESH)

    high, low = split(acc[...])
    scaled3 = jnp.concatenate([high, high, low], axis=0)
    blocks = [(i, j) for i in range(norb // BASE) for j in range(i + 1)]
    for i in range(norb // BASE):
        made = dot(turned3[i * BASE:(i + 1) * BASE, :], scaled3[:, :(i + 1) * BASE], ((1,), (0,)))
        made = made * (weight * weight)
        for j in range(i + 1):
            side_of, index = divmod(blocks.index((i, j)), len(blocks) // 2)
            part[side_of, index * BASE:(index + 1) * BASE, :] = made[:, j * BASE:(j + 1) * BASE]
    to_sibling = pltpu.make_async_remote_copy(
        src_ref=part.at[1 - core], dst_ref=half_buf, send_sem=half_sem.at[0], recv_sem=half_sem.at[1],
        device_id={"blk": sibling}, device_id_type=MESH)
    to_sibling.start()
    for j in range(1, n_grp):
        app_copy(j, 0).start()
    to_sibling.wait_recv()
    red[...] = (part[core] + half_buf[...]).reshape(red.shape)

    def rs_copy(j):
        to = (place + j) % chips
        return pltpu.make_async_remote_copy(
            src_ref=red.at[to], dst_ref=rs_buf.at[j], send_sem=rs_send.at[j], recv_sem=rs_recv.at[j],
            device_id={"blk": device_at(to, core)}, device_id_type=MESH)

    for j in range(1, chips):
        rs_copy(j).start()
    total = red[place]
    for j in range(1, chips):
        rs_copy(j).wait_recv()
        total = total + rs_buf[j]
    grp_buf[grp] = total

    def grp_copy(j):
        return pltpu.make_async_remote_copy(
            src_ref=grp_buf.at[grp], dst_ref=grp_buf.at[grp],
            send_sem=grp_send.at[j], recv_sem=grp_recv.at[grp],
            device_id={"grp": (grp + j) % n_grp}, device_id_type=MESH)

    def grp_in(j):
        other = (grp + j) % n_grp
        return pltpu.make_async_remote_copy(
            src_ref=grp_buf.at[other], dst_ref=grp_buf.at[other],
            send_sem=grp_send.at[j], recv_sem=grp_recv.at[other],
            device_id={"grp": other}, device_id_type=MESH)

    for j in range(1, n_grp):
        grp_copy(j).start()
    for h in range(1, PIECES):
        for j in range(1, n_grp):
            app_copy(j, h).start()
    for j in range(1, n_grp):
        grp_in(j).wait_recv()
    total = grp_buf[0]
    for j in range(1, n_grp):
        total = total + grp_buf[j]
    mine = core * chips + place
    corr_buf[mine] = total

    def ag_copy(block, sem, target):
        return pltpu.make_async_remote_copy(
            src_ref=corr_buf.at[block], dst_ref=corr_buf.at[block],
            send_sem=sem, recv_sem=ag_recv.at[block],
            device_id={"blk": target}, device_id_type=MESH)

    for j in range(1, chips):
        ag_copy(mine, ag_send.at[j], device_at(place + j, core)).start()
    ag_copy(mine, ag_sib.at[0], sibling).start()
    for j in range(1, chips):
        block = core * chips + (place + chips - j) % chips
        ag_copy(block, ag_sib.at[j], sibling).wait_recv()
        ag_copy(block, ag_sib.at[j], sibling).start()
    for j in range(chips):
        block = (1 - core) * chips + (place + chips - j) % chips
        ag_copy(block, ag_sib.at[j], sibling).wait_recv()
    factor(corr_buf[...].reshape(-1, BASE), a, inverses, work)

    for h in range(PIECES):
        for j in range(1, n_grp):
            app_in(j, h).wait_recv()
    whole = app_buf[0]
    for j in range(1, n_grp):
        whole = whole + app_buf[j]
    out_ref[...] = whole
    solve(out_ref, a, inverses)

    def sent(d, carry):
        for kind, sign, target in ((0, -1, right), (1, 1, left)):
            origin = device_at(place + sign * d, core)
            for h in range(PIECES):
                onward(d, h, kind, lambda: send(origin, h, kind, target).wait_send())
                send(origin, h, 2, sibling).wait_send()
        return carry

    lax.fori_loop(1, full + 1, sent, 0)
    for h in range(PIECES):
        send(me, h, 0, right).wait_send()
        send(me, h, 1, left).wait_send()
        send(me, h, 2, sibling).wait_send()
        send(across, h, 2, sibling).wait_send()
    to_sibling.wait_send()
    for j in range(1, chips):
        rs_copy(j).wait_send()
        ag_copy(mine, ag_send.at[j], device_at(place + j, core)).wait_send()
    for j in range(chips):
        block = core * chips + (place + chips - j) % chips
        ag_copy(block, ag_sib.at[j], sibling).wait_send()
    for j in range(1, n_grp):
        grp_copy(j).wait_send()
        for h in range(PIECES):
            app_copy(j, h).wait_send()


def split3(value):
    high = value.astype(BF16).astype(F32)
    rest = value - high
    middle = rest.astype(BF16).astype(F32)
    return high, middle, rest - middle


def diagonal_inverse(work):
    size = work.shape[0]
    sub = lax.broadcasted_iota(jnp.int32, (8, size), 0)
    lane = lax.broadcasted_iota(jnp.int32, (8, size), 1)

    def eliminate(top, both):
        count = 2 if both else 1
        left = [work[top + 8 * r:top + 8 * r + 8, :size] for r in range(count)]
        right = [work[top + 8 * r:top + 8 * r + 8, size:] for r in range(count)]
        cols = [[jnp.broadcast_to(left[r][:, top + j:top + j + 1], (8, size)) for j in range(8)] for r in range(count)]
        scale = jnp.ones((8, size), F32)
        for j in range(8):
            root = lax.rsqrt(jnp.broadcast_to(cols[0][j][j:j + 1, :], (8, size)))
            scale = jnp.where(sub == j, root, scale)
            inverse = root * root
            left_row, right_row = left[0][j:j + 1, :], right[0][j:j + 1, :]
            col_rows = [cols[0][m][j:j + 1, :] for m in range(8)]
            for r in range(count):
                factor = cols[r][j] * inverse
                if r == 0:
                    factor = jnp.where(sub > j, factor, 0.0)
                for m in range(j + 1, 8):
                    cols[r][m] = cols[r][m] - factor * col_rows[m]
                left[r] = left[r] - factor * left_row
                right[r] = right[r] - factor * right_row
        pivots_left, pivots_right = left[0] * scale, right[0] * scale
        work[top:top + 8, size:] = pivots_right
        if both:
            work[top + 8:top + 16, :size] = left[1]
            work[top + 8:top + 16, size:] = right[1]
        rest = top + 16
        if rest < size:
            below = jnp.where(lane >= rest, pivots_left, 0.0)
            bh, bm, bl = split3(below)
            ah, am, al = split3(jnp.concatenate([pivots_left, pivots_right], axis=1))
            near = jnp.concatenate([bh, bh, bm, bh, bl, bm], axis=0).astype(BF16)
            far = jnp.concatenate([ah, am, ah, al, ah, am], axis=0).astype(BF16)
            update = dot(near, far, ((0,), (0,)))
            work[rest:, :] -= update[rest:, :]

    for step in range(size // 8):
        eliminate(8 * step, 8 * step + 8 < size)


def factor(packed, a, inverses, work):
    norb, base = a.shape[0], BASE
    index = 0
    for i in range(norb // base):
        for j in range(i + 1):
            a[i * base:(i + 1) * base, j * base:(j + 1) * base] = packed[index * base:(index + 1) * base, :]
            index += 1
    eye = (lax.broadcasted_iota(jnp.int32, (base, base), 0)
           == lax.broadcasted_iota(jnp.int32, (base, base), 1)).astype(F32)
    for b in range(norb // base):
        here = slice(b * base, (b + 1) * base)
        work[:, :base] = a[here, here]
        work[:, base:] = eye
        diagonal_inverse(work)
        inverses[b] = work[:, base:]
        if (b + 1) * base == norb:
            break
        below = slice((b + 1) * base, norb)
        a[below, here] = lax.dot_general(
            a[below, here], inverses[b], (((1,), (1,)), ((), ())), precision=HIGHEST, preferred_element_type=F32)
        for j in range(b + 1, norb // base):
            low = slice(j * base, norb)
            there = slice(j * base, (j + 1) * base)
            a[low, there] -= lax.dot_general(
                a[low, here], a[there, here], (((1,), (1,)), ((), ())),
                precision=HIGHEST, preferred_element_type=F32)


def solve(x, a, inverses):
    norb, base = a.shape[0], BASE
    for b in range(norb // base):
        here = slice(b * base, (b + 1) * base)
        solved = lax.dot_general(
            x[:, here], inverses[b], (((1,), (1,)), ((), ())), precision=HIGHEST, preferred_element_type=F32)
        x[:, here] = solved
        if (b + 1) * base < norb:
            after = slice((b + 1) * base, norb)
            x[:, after] -= lax.dot_general(
                solved, a[after, here], (((1,), (1,)), ((), ())), precision=HIGHEST, preferred_element_type=F32)


def solution(mesh):
    n_blk, n_grp = mesh.shape["blk"], mesh.shape["grp"]
    inner_two = two_wide(mesh)
    chips = n_blk // 2

    def shards(orbitals, points):
        rows, norb = orbitals.shape
        weight = 1.0 / (rows * n_blk)
        width = rows // n_grp
        start = lax.axis_index("grp") * width
        far_rows = lax.dynamic_slice_in_dim(orbitals, start, width, 0)
        far_coords = lax.dynamic_slice_in_dim(points, start, width, 1)
        far_coords = jnp.pad(far_coords, ((0, PAD - 3), (0, norb - width)))
        own = jnp.concatenate([far_coords, far_rows], axis=0)
        packed = norb * (norb // BASE + 1) // 2
        share = packed // n_blk
        vmem = pl.BlockSpec(memory_space=pltpu.VMEM)
        dma = pltpu.SemaphoreType.DMA
        return pl.pallas_call(
            functools.partial(apply_kernel, (n_blk, n_grp, inner_two, weight, min(512, rows))),
            out_shape=jax.ShapeDtypeStruct((rows, norb), F32),
            in_specs=[vmem] * 3,
            out_specs=vmem,
            scratch_shapes=[
                pltpu.VMEM((n_blk, PAD + width, norb), F32),
                pltpu.VMEM((rows, 3 * norb), BF16),
                pltpu.VMEM((norb, 3 * rows), BF16),
                pltpu.VMEM((width, 3 * norb), BF16),
                pltpu.VMEM((3 * width, norb), BF16),
                pltpu.VMEM((rows, norb), F32),
                pltpu.VMEM((2, packed // 2, BASE), F32),
                pltpu.VMEM((packed // 2, BASE), F32),
                pltpu.VMEM((chips, share, BASE), F32),
                pltpu.VMEM((chips, share, BASE), F32),
                pltpu.VMEM((n_grp, share, BASE), F32),
                pltpu.VMEM((n_blk, share, BASE), F32),
                pltpu.VMEM((n_grp, rows, norb), F32),
                dma((n_blk, PIECES)), dma((3, n_blk, PIECES)), dma((2,)), dma((chips,)), dma((chips,)),
                dma((n_grp,)), dma((n_grp,)), dma((n_blk,)), dma((chips,)), dma((chips,)),
                dma((n_grp, PIECES)), dma((n_grp, PIECES)),
                pltpu.VMEM((norb, norb), F32),
                pltpu.VMEM((norb // BASE, BASE, BASE), F32),
                pltpu.VMEM((BASE, 2 * BASE), F32),
            ],
            compiler_params=pltpu.CompilerParams(
                collective_id=0, has_side_effects=True, vmem_limit_bytes=48 << 20),
            name="exchange_vectors",
        )(orbitals, own, points.T)

    return jax.shard_map(
        shards,
        mesh=mesh,
        in_specs=(P("blk", None), P(None, "blk")),
        out_specs=P("blk", None),
        check_vma=False,
    )
```
